32 devices in a mesh: row: 8 (over y, x, core), col: 4 (over z).
Axes of the slice: x: 2, y: 2, z: 4, core: 2. Of those that a mesh axis runs over, the one named last changes fastest.
Arguments:
- trailing: float32 [16384, 16384], P('row', 'col'), may hold values from -12 to 12, as said below
- panel: float32 [16384, 256], P('row'), may hold values from -3 to 3, as said below
Outputs:
- updated: float32 [16384, 16384], P('row', 'col')
- band_block: float32 [256, 256], replicated
The draws below stay inside these ranges and needn't reach their ends.
Inputs may be any that keep to these rules, and one draw needn't show every extreme that they name: trailing, read in global order, equals its transpose. Read in global order, the top 256 x 256 block of panel is 2 I plus entries of magnitude at most 6 / sqrt(16384), and the rows below have entries of magnitude at most 6 / sqrt(16384).
All inputs are finite; a program needn't handle non-finite values.
Results may differ from the reference program's by a relative error of at most 0.00011.
Values sent between devices are 32-bit elements; how exact they have to be, the bound alone decides.
A program may use at most 128 MiB of HBM per device.

```python
import jax
import jax.numpy as jnp
from jax import lax

M = 16384
NB = 256
LOCAL_ROWS = 2048
LOCAL_COLS = 4096
N_ROW = 8
N_COL = 4


def store_rows_drawn(matrix, groups):
    blocks = matrix.shape[0] // (NB * groups)
    return matrix.reshape(blocks, groups, NB, -1).transpose(1, 0, 2, 3).reshape(matrix.shape[0], -1)


def draw_trailing(key, part):
    base = jax.random.normal(key, (M, M), jnp.float32)
    symmetric = (base + base.T) * 0.7071
    return store_rows_drawn(store_rows_drawn(symmetric, M // LOCAL_ROWS).T, M // LOCAL_COLS).T


def draw_panel(key, part):
    first_key = jax.random.fold_in(key, 11)
    noise = jax.random.normal(first_key, (M, NB), jnp.float32)
    noise = jnp.clip(noise, -6.0, 6.0) / M ** 0.5
    diagonal = jnp.concatenate([2.0 * jnp.eye(NB, dtype=jnp.float32), jnp.zeros((M - NB, NB), jnp.float32)], axis=0)
    return store_rows_drawn(noise + diagonal, M // LOCAL_ROWS)


def setup_inputs(seed: int = 0) -> dict:
    arg_keys = jax.random.split(jax.random.key(seed), 3)
    return {
        "trailing": draw_trailing(jax.random.fold_in(arg_keys[2], 71), 0),
        "panel": draw_panel(jax.random.fold_in(arg_keys[2], 71), 0),
    }


def matmul(left, right):
    return jnp.dot(left.astype(jnp.float32), right.astype(jnp.float32), precision=lax.Precision.HIGHEST, preferred_element_type=jnp.float32)

def lu_unpivoted(matrix):
    order_size = matrix.shape[0]
    positions = jnp.arange(order_size)

    def eliminate(column, factors):
        below = positions > column
        pivot_value = factors[column, column]
        multipliers = jnp.where(below, factors[:, column] / pivot_value, 0.0)
        pivot_row = jnp.where(below, factors[column, :], 0.0)
        factors = factors - multipliers[:, None] * pivot_row[None, :]
        return factors.at[:, column].set(jnp.where(below, multipliers, factors[:, column]))
    factors = lax.fori_loop(0, order_size, eliminate, matrix)
    unit_lower = jnp.tril(factors, -1) + jnp.eye(order_size, dtype=matrix.dtype)
    return (unit_lower, jnp.triu(factors))

def unstore_rows(matrix, groups):
    blocks = matrix.shape[0] // (NB * groups)
    return matrix.reshape(groups, blocks, NB, -1).transpose(1, 0, 2, 3).reshape(matrix.shape[0], -1)

def store_rows(matrix, groups):
    blocks = matrix.shape[0] // (NB * groups)
    return matrix.reshape(blocks, groups, NB, -1).transpose(1, 0, 2, 3).reshape(matrix.shape[0], -1)

def reference(trailing, panel):
    full = unstore_rows(unstore_rows(trailing, N_ROW).T, N_COL).T
    column_block = unstore_rows(panel, N_ROW)
    identity = jnp.eye(NB, dtype=jnp.float32)
    gram_total = matmul(column_block.T, column_block)
    lower_chol = jnp.linalg.cholesky(gram_total)
    ortho_rows = jax.scipy.linalg.solve_triangular(lower_chol, column_block.T, lower=True).T
    unit_lower, upper_tri = lu_unpivoted(identity + ortho_rows[:NB])
    shifted = ortho_rows.at[:NB].add(identity)
    reflectors = jax.scipy.linalg.solve_triangular(upper_tri, shifted.T, trans='T', lower=False).T
    tri_factor = jax.scipy.linalg.solve_triangular(unit_lower, upper_tri.T, lower=True, unit_diagonal=True).T
    product = matmul(full, reflectors)
    inner_gram = matmul(reflectors.T, product)
    middle = matmul(matmul(tri_factor.T, inner_gram), tri_factor)
    update_rows = matmul(product, tri_factor) - 0.5 * matmul(reflectors, middle)
    result = full - matmul(reflectors, update_rows.T) - matmul(update_rows, reflectors.T)
    stored = store_rows(store_rows(result, N_ROW).T, N_COL).T
    return (stored, -lower_chol.T)
```

```python
import jax
import jax.numpy as jnp
from jax import lax
from jax.experimental import pallas as pl
from jax.experimental.pallas import tpu as pltpu
from jax.sharding import PartitionSpec as P

FULL = lax.Precision.HIGHEST
THREE = lax.Precision.HIGH
STEP = 64


def contract(left, right, dims, precision):
    return lax.dot_general(left, right, ((dims[:1], dims[1:]), ((), ())), precision=precision, preferred_element_type=jnp.float32)


def matmul(left, right, precision=FULL):
    return contract(left, right, (1, 0), precision)


def matmul_tn(left, right, precision=FULL):
    return contract(left, right, (0, 0), precision)


def matmul_nt(left, right, precision=FULL):
    return contract(left, right, (1, 1), precision)


def chol_kernel(gram_ref, upper_ref, work):
    size = gram_ref.shape[0]
    work[...] = gram_ref[...]
    sub = lax.broadcasted_iota(jnp.int32, (STEP, 2 * STEP), 0)
    lane = lax.broadcasted_iota(jnp.int32, (STEP, 2 * STEP), 1)
    eye = (lax.broadcasted_iota(jnp.int32, (STEP, STEP), 0) == lax.broadcasted_iota(jnp.int32, (STEP, STEP), 1)).astype(jnp.float32)
    row_pos = lax.broadcasted_iota(jnp.int32, (STEP, size), 0)
    col_pos = lax.broadcasted_iota(jnp.int32, (STEP, size), 1)
    for base in range(0, size, STEP):
        rows = work[base:base + STEP, :]
        pair = jnp.concatenate([rows[:, base:base + STEP], eye], axis=1)
        for j in range(STEP):
            col = jnp.broadcast_to(pair[:, j:j + 1], (STEP, 2 * STEP))
            pivot = col[j:j + 1, :]
            scale = lax.rsqrt(pivot)
            scale = scale * (1.5 - 0.5 * pivot * scale * scale)
            row = pair[j:j + 1, :] * scale
            reduced = pair - (col * scale) * row
            pair = jnp.where(sub > j, reduced, jnp.where(sub == j, row, pair))
        solved = matmul(pair[:, STEP:], rows)
        solved = jnp.where(col_pos >= row_pos + base, solved, 0.0)
        upper_ref[base:base + STEP, :] = solved
        if base + STEP < size:
            work[...] = work[...] - matmul_tn(solved, solved)


def inverse_kernel(matrix_ref, out_ref):
    size = matrix_ref.shape[0]
    out_ref[...] = matrix_ref[...]
    sub = lax.broadcasted_iota(jnp.int32, (STEP, STEP), 0)
    lane = lax.broadcasted_iota(jnp.int32, (STEP, STEP), 1)
    for base in range(0, size, STEP):
        rows = out_ref[base:base + STEP, :]
        block = rows[:, base:base + STEP]
        for j in range(STEP):
            col = jnp.broadcast_to(block[:, j:j + 1], (STEP, STEP))
            inv = 1.0 / col[j:j + 1, :]
            row = jnp.where(lane[:1] == j, inv, block[j:j + 1, :] * inv)
            rest = jnp.where(lane == j, 0.0, block) - col * row
            block = jnp.where(sub == j, row, rest)
        cols = out_ref[:, base:base + STEP]
        solved = matmul(block, rows)
        lanes = lax.broadcasted_iota(jnp.int32, (STEP, size), 1)
        inside = (lanes >= base) & (lanes < base + STEP)
        pieces = [jnp.zeros((STEP, STEP), jnp.float32)] * (size // STEP)
        pieces[base // STEP] = block
        solved = jnp.where(inside, jnp.concatenate(pieces, axis=1), solved)
        lanes = lax.broadcasted_iota(jnp.int32, (size, size), 1)
        kept = jnp.where((lanes >= base) & (lanes < base + STEP), 0.0, out_ref[...])
        out_ref[...] = kept - matmul(cols, solved)
        out_ref[base:base + STEP, :] = solved


def small_call(kernel, matrix, scratch, name):
    size = matrix.shape[0]
    return pl.pallas_call(
        kernel,
        out_shape=jax.ShapeDtypeStruct((size, size), jnp.float32),
        in_specs=[pl.BlockSpec(memory_space=pltpu.VMEM)],
        out_specs=pl.BlockSpec(memory_space=pltpu.VMEM),
        scratch_shapes=scratch,
        compiler_params=pltpu.CompilerParams(vmem_limit_bytes=16 * 1024 * 1024),
        cost_estimate=pl.CostEstimate(flops=40_000_000_000, bytes_accessed=8 * size * size, transcendentals=0),
        name=name,
    )(matrix)


def cholesky_upper(matrix):
    return small_call(chol_kernel, matrix, [pltpu.VMEM(matrix.shape, jnp.float32)], "cholesky_upper")


def inverse(matrix):
    return small_call(inverse_kernel, matrix, [], "block_inverse")


def mirror(row_piece, col_count, col_index, band_size):
    group_ratio = lax.axis_size("row") // col_count
    blocks = row_piece.shape[0] // band_size
    gathered = lax.all_gather(row_piece, "row", axis=0, tiled=True)
    gathered = gathered.reshape(group_ratio, col_count, blocks, band_size, band_size)
    pieces = lax.dynamic_index_in_dim(gathered, col_index, 1, keepdims=False)
    return pieces.transpose(1, 0, 2, 3).reshape(group_ratio * row_piece.shape[0], band_size)


def shards(trailing, panel):
    col_count = lax.axis_size("col")
    row_index = lax.axis_index("row")
    col_index = lax.axis_index("col")
    band_size = panel.shape[1]
    row_first = (row_index == 0).astype(jnp.float32)
    col_first = (col_index == 0).astype(jnp.float32)
    first = jnp.concatenate([matmul_tn(panel, panel), panel[:band_size] * row_first], axis=0)
    first = lax.psum(first, "row")
    gram_total, top_rows = first[:band_size], first[band_size:]
    panel_cols = mirror(panel, col_count, col_index, band_size)
    upper = cholesky_upper(gram_total)
    v_rows = panel.at[:band_size].add(upper * row_first)
    v_cols = panel_cols.at[:band_size].add(upper * col_first)
    part_cols = matmul_tn(trailing, v_rows, THREE)
    x_cols = lax.psum(part_cols, "row")
    part_rows = matmul(trailing, v_cols, THREE)
    x_rows = lax.psum(part_rows, "col")
    inner = lax.psum(matmul_tn(v_rows, part_rows), ("row", "col"))
    core = inverse(gram_total + matmul_tn(upper, top_rows))
    half = 0.5 * matmul_nt(matmul(core, inner), core)
    w_rows = matmul_nt(x_rows, core, THREE) - matmul(v_rows, half, THREE)
    w_cols = matmul_nt(x_cols, core, THREE) - matmul(v_cols, half, THREE)
    left = jnp.concatenate([v_rows, w_rows], axis=1)
    right = jnp.concatenate([w_cols, v_cols], axis=1)
    return (trailing - matmul_nt(left, right, THREE), -upper)


def solution(mesh):
    return jax.shard_map(
        shards,
        mesh=mesh,
        in_specs=(P("row", "col"), P("row", None)),
        out_specs=(P("row", "col"), P()),
        check_vma=False,
    )
```
